32 devices in a mesh: dp: 2 (over core), ctx: 8 (over z, x), tp: 2 (over y).
Axes of the slice: x: 2, y: 2, z: 4, core: 2. Of those that a mesh axis runs over, the one named last changes fastest.
Arguments:
- x_in: bfloat16 [2, 4096, 8192], P('dp', 'ctx', 'tp'), may hold values from -6 to 6
- grad_out: bfloat16 [2, 4096, 8192], P('dp', 'ctx', 'tp'), may hold values from -16 to 16
- state_maps: bfloat16 [2, 4096, 256], P('dp', 'ctx'), may hold values from -0.875 to 0.875
- dt_raw: float32 [2, 128, 4096], P('dp', 'tp', 'ctx'), may hold values from -3 to 20
- a_log: float32 [128], P('tp'), may hold values from -12 to 0
- saved_states: float32 [2, 8, 128, 64, 128], P('dp', 'ctx', 'tp'), may hold values from -0.625 to 0.625
- layer_in: bfloat16 [2, 4096, 8192], P('dp', 'ctx', 'tp'), may hold values from -40 to 40
- doc_lengths: int32 [2, 4], P('dp'), may hold values from 1 to 2048, 4096 in all within a row
Outputs:
- grad_x: bfloat16 [2, 4096, 8192], P('dp', 'ctx', 'tp')
- grad_maps: float32 [2, 4096, 256], P('dp', ('ctx', 'tp'))
- grad_dt_proj: float32 [128, 8192], P(('dp', 'ctx'), 'tp')
The draws below stay inside these ranges and needn't reach their ends.
All inputs are finite; a program needn't handle non-finite values.
Results may differ from the reference program's by a relative error of at most 0.0055.
Values may be sent and summed in bfloat16 or wider, within the bound.
A program may use at most 128 MiB of HBM per device.

```python
import math
import jax
import jax.numpy as jnp
import numpy as np
from jax import lax

D = 8192
HEADS = 128
HEAD_DIM = 64
STATE = 128
TOK_DEV = 512
DOCS = 4
BATCH_SEQUENCES = 2
BLOCKS = 8
SEQUENCE_LENGTH = 4096


def decay_plan(key):
    random_subkey_list = jax.random.split(key, 4)
    slow_share = 0.5
    slow_heads = jax.random.uniform(random_subkey_list[0], (HEADS,)) < slow_share
    slow_rate = jnp.exp(jax.random.uniform(random_subkey_list[1], (HEADS,), minval=math.log(0.2), maxval=math.log(0.8))) / SEQUENCE_LENGTH
    fast_rate = jnp.exp(jax.random.uniform(random_subkey_list[2], (HEADS,), minval=math.log(0.02), maxval=math.log(0.05)))
    decay_rate = jnp.where(slow_heads, slow_rate, fast_rate)
    default_step_size = jnp.exp(jax.random.uniform(random_subkey_list[3], (HEADS,), minval=math.log(0.2), maxval=math.log(0.6)))
    return (decay_rate, default_step_size)


def draw_a_log(key, part):
    decay_rate, default_step_size = decay_plan(jax.random.fold_in(key, 11))
    return jnp.log(decay_rate / default_step_size).astype(jnp.float32)


def draw_dt_raw(key, part):
    decay_rate, default_step_size = decay_plan(jax.random.fold_in(key, 11))
    random_subkey_list = jax.random.split(jax.random.fold_in(key, 12), 3)
    block_count = SEQUENCE_LENGTH // TOK_DEV
    block_multiplier = jnp.exp(jax.random.uniform(random_subkey_list[0], (BATCH_SEQUENCES, HEADS, block_count), minval=-math.log(2.0), maxval=math.log(2.0)))
    block_multiplier = jnp.repeat(block_multiplier, TOK_DEV, axis=2)
    token_multiplier = jnp.exp(jax.random.uniform(random_subkey_list[1], (BATCH_SEQUENCES, HEADS, SEQUENCE_LENGTH), minval=-math.log(2.0), maxval=math.log(2.0)))
    spike_events = jax.random.uniform(random_subkey_list[2], (BATCH_SEQUENCES, 1, SEQUENCE_LENGTH)) < 4.0 / SEQUENCE_LENGTH
    spike_increase = jnp.where(spike_events, 8.0, 1.0)
    step_sizes_delta = default_step_size[None, :, None] * block_multiplier * token_multiplier * spike_increase
    return jnp.log(jnp.expm1(step_sizes_delta)).astype(jnp.float32)


def draw_grad_out(key, part):
    columns = HEADS * HEAD_DIM
    head_index = (jnp.arange(columns) // HEAD_DIM).astype(jnp.float32)
    random_subkey_list = jax.random.split(key, 1)
    head_scale = 0.5 * (1.0 + 2.0 * head_index / (HEADS - 1))
    drawn = jax.random.truncated_normal(random_subkey_list[0], -4.0, 4.0, (BATCH_SEQUENCES, SEQUENCE_LENGTH, columns)) * head_scale
    return drawn.astype(jnp.bfloat16)


def draw_layer_in(key, part):
    fraction = jnp.arange(D).astype(jnp.float32) / D
    random_subkey_list = jax.random.split(key, 1)
    column_scale = 0.3 * jnp.power(10.0, fraction)
    drawn = jax.random.truncated_normal(random_subkey_list[0], -4.0, 4.0, (BATCH_SEQUENCES, SEQUENCE_LENGTH, D)) * column_scale
    return drawn.astype(jnp.bfloat16)


def block_levels(rng, dims, cuts, low, high):
    level, own = 1.0, jax.random.fold_in(rng, 6)
    for axis_at, blocks in cuts:
        steps = jnp.exp(jax.random.uniform(jax.random.fold_in(own, axis_at), (blocks,), jnp.float32, low / len(cuts), high / len(cuts)))
        level = level * jnp.repeat(steps, dims[axis_at] // blocks).reshape([-1 if axis == axis_at else 1 for axis in range(len(dims))])
    return level


def split_up(count, total, reach, slope):
    weights = [(1 << 20) // math.isqrt(grade ** slope) + 1 for grade in range(2, count + 1)]
    surplus, given = total - reach - (count - 1), [1] * (count - 1)
    while surplus > 0:
        candidates = [i for i in range(count - 1) if given[i] < reach]
        whole, remaining = sum([weights[i] for i in candidates]), surplus
        for i in candidates:
            more = min(reach - given[i], max(1, remaining * weights[i] // whole), surplus)
            given[i] = given[i] + more
            surplus = surplus - more
    return np.array([reach] + given)


def uneven_parts(own_key, count, total, most, slope):
    if count == 2:
        one = jax.random.randint(own_key, (), max(1, total - most), min(most, total - 1) + 1)
        return jnp.stack([one, total - one])
    lengths = jnp.asarray(split_up(count, total, most, slope), jnp.int32)
    pairs = (count - 1) // 2
    donor, taker = lengths[1:1 + 2 * pairs:2], lengths[2:2 + 2 * pairs:2]
    margin = jnp.minimum(donor - 1, most - taker)
    moved = jax.random.randint(jax.random.fold_in(own_key, 1), (pairs,), 0, 1 << 20) % (margin + 1)
    lengths = lengths.at[1:1 + 2 * pairs:2].set(donor - moved).at[2:2 + 2 * pairs:2].set(taker + moved)
    return lengths[jax.random.permutation(jax.random.fold_in(own_key, 2), count)]


def gaussian(key, extent, deviation, reach, pieces=(), kind=jnp.bfloat16):
    entries = jax.random.normal(key, extent, jnp.float32) * deviation
    if len(pieces) > 0:
        entries = block_levels(key, extent, pieces, -0.22, 0.18) * entries
    return jnp.clip(entries, min=-reach, max=reach).astype(kind)


def setup_inputs(seed: int = 0) -> dict:
    seeds = jax.random.split(jax.random.key(seed), 9)
    return {
        "x_in": gaussian(seeds[0], (BATCH_SEQUENCES, SEQUENCE_LENGTH, HEADS * HEAD_DIM), 1.0, 6.0, ((0, 2), (1, 8), (2, 2))),
        "grad_out": draw_grad_out(jax.random.fold_in(seeds[8], 71), 0),
        "state_maps": gaussian(seeds[2], (BATCH_SEQUENCES, SEQUENCE_LENGTH, 2 * STATE), 0.15, 0.875, ((0, 2), (1, 8))),
        "dt_raw": draw_dt_raw(jax.random.fold_in(seeds[8], 71), 0),
        "a_log": draw_a_log(jax.random.fold_in(seeds[8], 71), 0),
        "saved_states": gaussian(seeds[5], (BATCH_SEQUENCES, BLOCKS, HEADS, HEAD_DIM, STATE), 0.1, 0.625, ((0, 2), (1, 8), (2, 2)), jnp.float32),
        "layer_in": draw_layer_in(jax.random.fold_in(seeds[8], 71), 0),
        "doc_lengths": jax.vmap(lambda own: uneven_parts(own, DOCS, SEQUENCE_LENGTH, SEQUENCE_LENGTH // 2, 2))(jax.random.split(seeds[7], BATCH_SEQUENCES)).reshape((BATCH_SEQUENCES, DOCS)).astype(jnp.int32),
    }


head_group = 4
epsilon = 1e-06

def block_setup(raw_steps, a_log, labels, before):
    step_sizes_delta = jax.nn.softplus(raw_steps)
    decay_rate = -jnp.exp(a_log)
    cumulative = jnp.cumsum(decay_rate[:, None] * step_sizes_delta, axis=1)
    enter_w = jnp.exp(cumulative) * (labels == before).astype(jnp.float32)[None, :]
    leave_w = jnp.exp(cumulative[:, -1:] - cumulative) * (labels == labels[-1]).astype(jnp.float32)[None, :]
    return (step_sizes_delta, decay_rate, cumulative, enter_w, leave_w)

def first_pass(dy_rows, c_rows, enter_w):
    scaled = (jnp.transpose(enter_w)[:, :, None] * dy_rows.astype(jnp.float32)).astype(jnp.bfloat16)
    local_grad = jnp.einsum('ihp,in->hpn', scaled.astype(jnp.float32), c_rows.astype(jnp.float32), precision=lax.Precision.HIGHEST)
    return (scaled, local_grad)

def quad_terms(cumulative, step_sizes_delta, x_rows, dy_rows, pair_dot, causal):
    length, head_count, head_width = x_rows.shape
    highest = lax.Precision.HIGHEST

    def one_group(group_index, running):
        mixed_sum, r_local, dc_local = running
        offset = group_index * head_group
        c_part = lax.dynamic_slice_in_dim(cumulative, offset, head_group, 0)
        d_part = lax.dynamic_slice_in_dim(step_sizes_delta, offset, head_group, 0)
        x_part = lax.dynamic_slice_in_dim(x_rows, offset, head_group, 1)
        y_part = lax.dynamic_slice_in_dim(dy_rows, offset, head_group, 1)
        log_diffs = c_part[:, :, None] - c_part[:, None, :]
        kernel = jnp.where(causal[None], jnp.exp(jnp.where(causal[None], log_diffs, 0.0)), 0.0)
        weighted = kernel * pair_dot[None]
        rounded = weighted.astype(jnp.bfloat16)
        inner_dt = jnp.einsum('ihp,jhp->hij', y_part.astype(jnp.float32), x_part.astype(jnp.float32), precision=highest) * d_part[:, None, :]
        r_part = jnp.einsum('hij,ihp->jhp', rounded.astype(jnp.float32), y_part.astype(jnp.float32), precision=highest)
        products = weighted * inner_dt
        dc_part = lax.optimization_barrier(jnp.sum(products, axis=2)) - lax.optimization_barrier(jnp.sum(products, axis=1))
        mixed_sum = mixed_sum + lax.optimization_barrier(jnp.sum(kernel * inner_dt, axis=0))
        r_local = lax.dynamic_update_slice_in_dim(r_local, r_part, offset, 1)
        dc_local = lax.dynamic_update_slice_in_dim(dc_local, dc_part, offset, 0)
        return (mixed_sum, r_local, dc_local)
    initial = (jnp.zeros((length, length), jnp.float32), jnp.zeros((length, head_count, head_width), jnp.float32), jnp.zeros((head_count, length), jnp.float32))
    return lax.fori_loop(0, head_count // head_group, one_group, initial)

def block_grads(x_rows, dy_rows, map_rows, raw_steps, labels, before, states, carried, a_log):
    highest = lax.Precision.HIGHEST
    length = x_rows.shape[0]
    b_rows = map_rows[:, :STATE].astype(jnp.float32)
    c_rows = map_rows[:, STATE:].astype(jnp.float32)
    step_sizes_delta, decay_rate, cumulative, enter_w, leave_w = block_setup(raw_steps, a_log, labels, before)
    scaled, local_grad = first_pass(dy_rows, map_rows[:, STATE:], enter_w)
    positions = jnp.arange(length)
    causal = (positions[:, None] >= positions[None, :]) & (labels[:, None] == labels[None, :])
    pair_dot = jnp.dot(c_rows, b_rows.T, preferred_element_type=jnp.float32, precision=highest)
    mixed_sum, r_local, dc_local = quad_terms(cumulative, step_sizes_delta, x_rows, dy_rows, pair_dot, causal)
    state_term = jnp.einsum('ihp,hpn->in', scaled.astype(jnp.float32), states, precision=highest)
    local_b = jnp.einsum('ij,in->jn', mixed_sum, c_rows, precision=highest)
    local_c = jnp.einsum('ij,jn->in', mixed_sum, b_rows, precision=highest) + state_term
    state_c = jnp.einsum('in,hpn->ihp', c_rows, states, precision=highest)
    enter_out = enter_w * jnp.einsum('ihp,ihp->hi', dy_rows.astype(jnp.float32), state_c, precision=highest)
    carry_b = jnp.einsum('jn,hpn->jhp', b_rows, carried, precision=highest)
    carry_r = jnp.transpose(leave_w)[:, :, None] * carry_b
    r_all = r_local + carry_r
    x_wide = x_rows.astype(jnp.float32)
    weighted_x = jnp.transpose(step_sizes_delta * leave_w)[:, :, None] * x_wide
    carry_bgrad = jnp.einsum('jhp,hpn->jn', weighted_x, carried, precision=highest)
    grad_x = (jnp.transpose(step_sizes_delta)[:, :, None] * r_all).astype(jnp.bfloat16)
    w_term = step_sizes_delta * jnp.einsum('jhp,jhp->hj', x_wide, carry_r, precision=highest)
    v_term = enter_w[:, -1] * lax.optimization_barrier(jnp.sum(carried * states, axis=(1, 2)))
    last_mask = (positions == length - 1).astype(jnp.float32)
    cum_grad = dc_local + enter_out - w_term + (v_term + lax.optimization_barrier(jnp.sum(w_term, axis=1)))[:, None] * last_mask[None, :]
    tail_sum = jnp.flip(jnp.cumsum(jnp.flip(cum_grad, 1), axis=1), 1)
    step_grad = jnp.einsum('jhp,jhp->hj', x_wide, r_all, precision=highest) + decay_rate[:, None] * tail_sum
    dt_grad = (step_grad * jax.nn.sigmoid(raw_steps)).astype(jnp.bfloat16)
    grad_maps = jnp.concatenate([local_b + carry_bgrad, local_c], axis=1)
    return (grad_x.reshape(length, -1), grad_maps, dt_grad)

def reference(x_in, grad_out, state_maps, dt_raw, a_log, saved_states, layer_in, doc_lengths):
    grads_x = []
    grads_maps = []
    dt_grads = []
    for replica in range(BATCH_SEQUENCES):
        doc_ends = jnp.cumsum(doc_lengths[replica]).astype(jnp.int32)
        positions = jnp.arange(SEQUENCE_LENGTH, dtype=jnp.int32)
        labels_all = lax.optimization_barrier(jnp.sum((positions[:, None] >= doc_ends[None, :]).astype(jnp.int32), axis=1)).astype(jnp.int32)
        prior_label = jnp.concatenate([jnp.full((1,), -1, jnp.int32), labels_all[:-1]])
        x_blocks = x_in[replica].reshape(BLOCKS, TOK_DEV, HEADS, HEAD_DIM)
        dy_blocks = grad_out[replica].reshape(BLOCKS, TOK_DEV, HEADS, HEAD_DIM)
        map_blocks = state_maps[replica].reshape(BLOCKS, TOK_DEV, 2 * STATE)
        raw_blocks = jnp.transpose(dt_raw[replica].reshape(HEADS, BLOCKS, TOK_DEV), (1, 0, 2))
        label_blocks = labels_all.reshape(BLOCKS, TOK_DEV)
        before_all = prior_label.reshape(BLOCKS, TOK_DEV)[:, 0]

        def section_one(payload):
            dy_rows, map_rows, raw_steps, labels, before = payload
            step_sizes_delta, decay_rate, cumulative, enter_w, leave_w = block_setup(raw_steps, a_log, labels, before)
            scaled, local_grad = first_pass(dy_rows, map_rows[:, STATE:], enter_w)
            return (enter_w[:, -1], local_grad)
        decay_ends, local_grads = lax.map(section_one, (dy_blocks, map_blocks, raw_blocks, label_blocks, before_all))

        def link_back(carried, payload):
            decay_end, local_grad = payload
            return (local_grad + decay_end[:, None, None] * carried, carried)
        zero_state = jnp.zeros((HEADS, HEAD_DIM, STATE), jnp.float32)
        unused, carries = lax.scan(link_back, zero_state, (decay_ends, local_grads), reverse=True)

        def section_two(payload):
            x_rows, dy_rows, map_rows, raw_steps, labels, before, states, carried = payload
            return block_grads(x_rows, dy_rows, map_rows, raw_steps, labels, before, states, carried, a_log)
        block_x, block_maps, block_dt = lax.map(section_two, (x_blocks, dy_blocks, map_blocks, raw_blocks, label_blocks, before_all, saved_states[replica], carries))
        grads_x.append(block_x.reshape(SEQUENCE_LENGTH, HEADS * HEAD_DIM))
        grads_maps.append(block_maps.reshape(SEQUENCE_LENGTH, 2 * STATE))
        dt_grads.append(block_dt)
    grad_x = jnp.stack(grads_x)
    grad_maps = jnp.stack(grads_maps)
    dt_all = jnp.stack(dt_grads).reshape(BATCH_SEQUENCES * BLOCKS, HEADS, TOK_DEV)
    layer_blocks = layer_in.reshape(BATCH_SEQUENCES * BLOCKS, TOK_DEV, D)

    def accumulate(running, payload):
        dt_part, layer_part = payload
        added = jnp.dot(dt_part.astype(jnp.float32), layer_part.astype(jnp.float32), preferred_element_type=jnp.float32, precision=lax.Precision.HIGHEST)
        return (running + added, None)
    summed, unused = lax.scan(accumulate, jnp.zeros((HEADS, D), jnp.float32), (dt_all, layer_blocks))
    norms = jnp.sqrt(lax.optimization_barrier(jnp.sum(summed * summed, axis=1)) + epsilon)
    target = jnp.mean(norms)
    grad_dt_proj = summed * jnp.minimum(1.0, target / norms)[:, None]
    return (grad_x, grad_maps, grad_dt_proj)
```

```python
import functools

import jax
import jax.numpy as jnp
from jax import lax
from jax.experimental import pallas as pl
from jax.experimental.pallas import tpu as pltpu
from jax.sharding import PartitionSpec as P

HEAD_DIM = 64
STATE = 128
PAIR = 2 * HEAD_DIM
TILE = 256
CHUNK = 64
epsilon = 1e-06
LOG2E = 1.4426950408889634
f32, bf16 = jnp.float32, jnp.bfloat16


def mm(a, b, ca, cb):
    return lax.dot_general(a, b, (((ca,), (cb,)), ((), ())), preferred_element_type=f32)


def spread(cols, first, second, rows):
    lane = lax.broadcasted_iota(jnp.int32, (rows, PAIR), 1)
    return jnp.where(lane < HEAD_DIM, cols[:, first : first + 1], cols[:, second : second + 1])


def head_sums(value, pair):
    high = value.astype(bf16)
    low = (value - high.astype(f32)).astype(bf16)
    row = lax.broadcasted_iota(jnp.int32, (2 * PAIR, 128), 0) % PAIR
    col = lax.broadcasted_iota(jnp.int32, (2 * PAIR, 128), 1)
    chosen = col == 2 * pair + jnp.where(row >= HEAD_DIM, 1, 0)
    return mm(jnp.concatenate([high, low], axis=1), jnp.where(chosen, 1.0, 0.0).astype(bf16), 1, 0)


def enter_kernel(pairs, aux_ref, dy_ref, c_ref, s_ref, local_ref, sterm_ref, eo_ref):
    step = pl.program_id(0)

    @pl.when(step == 0)
    def _():
        sterm_ref[...] = jnp.zeros_like(sterm_ref)
        eo_ref[...] = jnp.zeros_like(eo_ref)

    rows = dy_ref.shape[0]
    c_rows = c_ref[...]
    for p in range(pairs):
        at = slice(p * PAIR, (p + 1) * PAIR)
        cols = aux_ref[p].T
        wide = dy_ref[:, at].astype(f32) * spread(cols, 6, 7, rows)
        scaled = wide.astype(bf16)
        local_ref[at, :] = mm(scaled, c_rows, 0, 0).astype(bf16)
        state = s_ref[at, :].astype(bf16)
        sterm_ref[...] += mm(scaled, state, 1, 0)
        eo_ref[...] += head_sums(wide * mm(c_rows, state, 1, 1), step * pairs + p)


def quad_kernel(
    pairs, aux_ref, x_ref, dy_ref, b_ref, c_ref, labr_ref, labc_ref, *refs
):
    min_ref = refs[0] if len(refs) > 4 else None
    r_ref, a_ref, msum_ref, cb_ref = refs[-4:]
    length = x_ref.shape[0]

    @pl.when(pl.program_id(0) == 0)
    def _():
        at_j = lax.broadcasted_iota(jnp.int32, (length, length), 0)
        at_i = lax.broadcasted_iota(jnp.int32, (length, length), 1)
        keep = (at_i >= at_j) & (labc_ref[...] == labr_ref[...])
        cb_ref[...] = jnp.where(keep, mm(b_ref[...], c_ref[...], 1, 1), 0.0)
        msum_ref[...] = jnp.zeros_like(msum_ref) if min_ref is None else min_ref[...]

    blocks = length // TILE
    lane = lax.broadcasted_iota(jnp.int32, (length, PAIR), 1)
    for p in range(pairs):
        at = slice(p * PAIR, (p + 1) * PAIR)
        aux = aux_ref[p]
        cols = aux.T
        x = x_ref[:, at]
        dy = dy_ref[:, at]
        zero = jnp.zeros_like(dy)
        dys = (jnp.where(lane < HEAD_DIM, dy, zero), jnp.where(lane < HEAD_DIM, zero, dy))
        sums = [[jnp.zeros((8, TILE), f32) for _ in range(blocks)] for _ in range(2)]
        for jb in range(blocks):
            j0 = jb * TILE
            weights, sources = [], []
            for ib in range(jb, blocks):
                i0 = ib * TILE
                inner = [mm(x[j0 : j0 + TILE], dys[s][i0 : i0 + TILE], 1, 1) for s in range(2)]
                pieces = [[], []]
                for c in range(TILE // CHUNK):
                    lo = c * CHUNK
                    rows = slice(j0 + lo, j0 + lo + CHUNK)
                    cb = cb_ref[rows, i0 : i0 + TILE]
                    total = None
                    for s in range(2):
                        power = aux[s : s + 1, i0 : i0 + TILE] - cols[rows, 2 + s : 3 + s]
                        if ib == jb:
                            power = jnp.minimum(power, 16.0)
                        decay = jnp.exp2(power)
                        pieces[s].append((decay * cb).astype(bf16))
                        mixed = decay * inner[s][lo : lo + CHUNK]
                        total = mixed if total is None else total + mixed
                        product = (mixed * cb).reshape(CHUNK // 8, 8, TILE)
                        sums[s][ib] = sums[s][ib] + jnp.sum(product, axis=0)
                    msum_ref[rows, i0 : i0 + TILE] += total
                for s in range(2):
                    weights.append(jnp.concatenate(pieces[s], axis=0))
                    sources.append(dys[s][i0 : i0 + TILE])
            r_ref[j0 : j0 + TILE, at] = mm(
                jnp.concatenate(weights, axis=1), jnp.concatenate(sources, axis=0), 1, 0
            )
        for s in range(2):
            for ib in range(blocks):
                a_ref[0, 2 * p + s : 2 * p + s + 1, ib * TILE : (ib + 1) * TILE] = jnp.sum(
                    sums[s][ib], axis=0, keepdims=True
                )


def leave_kernel(
    pairs, aux_ref, x_ref, r_ref, b_ref, carry_ref, s_ref, gx_ref, u_ref, bgrad_ref, vw_ref
):
    step = pl.program_id(0)

    @pl.when(step == 0)
    def _():
        u_ref[...] = jnp.zeros_like(u_ref)
        bgrad_ref[...] = jnp.zeros_like(bgrad_ref)

    rows = x_ref.shape[0]
    for p in range(pairs):
        at = slice(p * PAIR, (p + 1) * PAIR)
        cols = aux_ref[p].T
        weight = spread(cols, 4, 5, rows)
        carry = carry_ref[at, :]
        x = x_ref[:, at].astype(f32)
        after = weight * mm(b_ref[...], carry, 1, 1)
        grad = r_ref[:, at] + after
        gx_ref[:, at] = grad.astype(bf16)
        u_ref[...] += head_sums(x * grad, step * pairs + p)
        bgrad_ref[...] += mm((weight * x).astype(bf16), carry, 1, 0)
        both = carry.astype(f32) * s_ref[at, :]
        vw_ref[p, 0:1, :] = jnp.sum(both[:HEAD_DIM], axis=0, keepdims=True)
        vw_ref[p, 1:2, :] = jnp.sum(both[HEAD_DIM:], axis=0, keepdims=True)
        vw_ref[p, 2:3, :] = jnp.sum(x * after, axis=0, keepdims=True)
        vw_ref[p, 3:8, :] = jnp.zeros((5, STATE), f32)


def segments(lengths_row, anchor, length):
    doc_ends = jnp.cumsum(lengths_row)
    positions = anchor + jnp.arange(length, dtype=jnp.int32)
    labels = jnp.sum((positions[:, None] >= doc_ends[None, :]).astype(jnp.int32), axis=1)
    before = jnp.sum((anchor - 1 >= doc_ends).astype(jnp.int32))
    before = jnp.where(anchor > 0, before, -1)
    return (labels, before)


def full(shape):
    return pl.BlockSpec(shape, lambda g: (0,) * len(shape))


def shift(value, back, count):
    if back >= count:
        return jax.tree.map(jnp.zeros_like, value)
    moves = [(k, k - back) for k in range(back, count)]
    return jax.tree.map(lambda part: lax.ppermute(part, "ctx", moves), value)


def shards(x_in, grad_out, state_maps, dt_raw, a_log, saved_states, layer_in, doc_lengths):
    high = lax.Precision.HIGHEST
    length, width = x_in.shape[1:]
    head_count = a_log.shape[0]
    pair_count = head_count // 2
    x_rows, dy_rows = x_in[0], grad_out[0]
    b_half = state_maps[0, :, :STATE]
    c_half = state_maps[0, :, STATE:]
    raw_steps = dt_raw[0]
    states = saved_states.reshape(width, STATE)
    count = lax.axis_size("ctx")
    anchor = lax.axis_index("ctx") * length
    labels, before = segments(doc_lengths[0], anchor, length)
    positions = jnp.arange(length)
    upto = (positions[:, None] <= positions[None, :]).astype(f32)
    steps = jax.nn.softplus(raw_steps)
    decay_rate = -jnp.exp(a_log)
    cumulative = jnp.dot(decay_rate[:, None] * steps, upto, precision=high)
    enter_w = jnp.exp(cumulative) * (labels == before).astype(f32)[None, :]
    leave_w = jnp.exp(cumulative[:, -1:] - cumulative) * (labels == labels[-1]).astype(f32)[None, :]
    scaled_cum = cumulative * LOG2E
    aux = jnp.stack([scaled_cum, scaled_cum - jnp.log2(steps), steps * leave_w, enter_w])
    aux = aux.reshape(4, pair_count, 2, length).transpose(1, 0, 2, 3)
    aux = aux.reshape(pair_count, 8, length)
    ends = enter_w[:, -1]

    wide_pairs = 4
    groups = pair_count // wide_pairs
    aux_spec = pl.BlockSpec((wide_pairs, 8, length), lambda g: (g, 0, 0))
    col_spec = pl.BlockSpec((length, wide_pairs * PAIR), lambda g: (0, g))
    row_spec = pl.BlockSpec((wide_pairs * PAIR, STATE), lambda g: (g, 0))
    limit = pltpu.CompilerParams(vmem_limit_bytes=40 * 1024 * 1024)
    local, state_term, enter_out = pl.pallas_call(
        functools.partial(enter_kernel, wide_pairs),
        grid=(groups,),
        in_specs=[aux_spec, col_spec, full((length, STATE)), row_spec],
        out_specs=[row_spec, full((length, STATE)), full((length, 128))],
        out_shape=[
            jax.ShapeDtypeStruct((width, STATE), bf16),
            jax.ShapeDtypeStruct((length, STATE), f32),
            jax.ShapeDtypeStruct((length, 128), f32),
        ],
        compiler_params=limit,
        name="enter",
    )(aux, dy_rows, c_half, states)

    odd = lax.axis_index("ctx") % 2
    half = head_count // 2
    swap = [(k, k ^ 1) for k in range(count)]

    def take(value, which):
        return lax.dynamic_index_in_dim(value, which, 0, keepdims=False)

    whole_local = local.reshape(2, half, HEAD_DIM * STATE)
    half_ends = ends.reshape(2, half)
    mine, mine_end = take(whole_local, odd), take(half_ends, odd)
    other = lax.ppermute(take(whole_local, 1 - odd), "ctx", swap)
    other_end = lax.ppermute(take(half_ends, 1 - odd), "ctx", swap)
    first = jnp.where(odd == 0, mine, other).astype(f32)
    second = jnp.where(odd == 0, other, mine).astype(f32)
    first_end = jnp.where(odd == 0, mine_end, other_end)
    group = (first + first_end[:, None] * second).astype(bf16)
    group_end = mine_end * other_end
    reach, window = 1, max(count // 4, 1)
    while reach < window:
        ahead, ahead_end = shift((group, group_end), 2 * reach, count)
        group = (group.astype(f32) + group_end[:, None] * ahead.astype(f32)).astype(bf16)
        group_end = group_end * ahead_end
        reach *= 2
    after = shift(group, 2, count)
    even_end = jnp.where(odd == 0, other_end, mine_end)
    even_after = (second + even_end[:, None] * after.astype(f32)).astype(bf16)
    back = lax.ppermute(jnp.where(odd == 0, after, even_after), "ctx", swap)
    kept = jnp.where(odd == 0, even_after, after)
    carry = jnp.where(odd == 0, jnp.stack([kept, back]), jnp.stack([back, kept]))
    carry = carry.reshape(width, STATE)

    quad_pairs = 2
    parts = 4 if pair_count % (4 * quad_pairs) == 0 else 1
    quad_groups = pair_count // quad_pairs // parts
    labr, labc = labels[None, :], labels[:, None]
    mixed = r_local = None
    a_parts = []
    for part in range(parts):
        base = part * quad_groups
        quad_spec = pl.BlockSpec((length, quad_pairs * PAIR), lambda g, base=base: (0, base + g))
        r_local, a_part, mixed = pl.pallas_call(
            functools.partial(quad_kernel, quad_pairs),
            grid=(quad_groups,),
            in_specs=[
                pl.BlockSpec((quad_pairs, 8, length), lambda g, base=base: (base + g, 0, 0)),
                quad_spec,
                quad_spec,
                full((length, STATE)),
                full((length, STATE)),
                full((1, length)),
                full((length, 1)),
            ]
            + ([full((length, length)), pl.BlockSpec(memory_space=pl.ANY)] if part else []),
            out_specs=[
                quad_spec,
                pl.BlockSpec((1, 2 * quad_pairs, length), lambda g: (g, 0, 0)),
                full((length, length)),
            ],
            out_shape=[
                jax.ShapeDtypeStruct((length, width), f32),
                jax.ShapeDtypeStruct((quad_groups, 2 * quad_pairs, length), f32),
                jax.ShapeDtypeStruct((length, length), f32),
            ],
            scratch_shapes=[pltpu.VMEM((length, length), f32)],
            input_output_aliases={8: 0} if part else {},
            compiler_params=limit,
            cost_estimate=pl.CostEstimate(
                flops=50_000_000_000 // parts, bytes_accessed=20_000_000 // parts, transcendentals=0
            ),
            name="quad",
        )(aux, x_rows, dy_rows, b_half, c_half, labr, labc, *([mixed, r_local] if part else []))
        a_parts.append(a_part.reshape(-1, length))
    a_sum = jnp.concatenate(a_parts, axis=0)
    keep = (positions[:, None] <= positions[None, :]) & (labc == labr)
    mixed = jnp.where(keep, mixed, 0.0).astype(bf16)
    local_b = jnp.dot(mixed, c_half, preferred_element_type=f32)
    local_c = mm(mixed, b_half, 0, 0) + state_term

    grad_x, u_sum, bgrad, vw = pl.pallas_call(
        functools.partial(leave_kernel, wide_pairs),
        grid=(groups,),
        in_specs=[aux_spec, col_spec, col_spec, full((length, STATE)), row_spec, row_spec],
        out_specs=[
            col_spec,
            full((length, 128)),
            full((length, STATE)),
            pl.BlockSpec((wide_pairs, 8, STATE), lambda g: (g, 0, 0)),
        ],
        out_shape=[
            jax.ShapeDtypeStruct((length, width), bf16),
            jax.ShapeDtypeStruct((length, 128), f32),
            jax.ShapeDtypeStruct((length, STATE), f32),
            jax.ShapeDtypeStruct((pair_count, 8, STATE), f32),
        ],
        compiler_params=limit,
        name="leave",
    )(aux, x_rows, r_local, b_half, carry, states)
    v_term = ends * jnp.sum(vw[:, 0:2], axis=2).reshape(head_count)
    w_sum = jnp.sum(vw[:, 2].reshape(head_count, HEAD_DIM), axis=1)
    u_rows = u_sum[:, :head_count].T
    cum_grad = a_sum + enter_out[:, :head_count].T - u_rows
    tail_sum = mm_high(cum_grad, upto, high) + (v_term + w_sum)[:, None]
    step_grad = u_rows / steps + decay_rate[:, None] * tail_sum
    dt_grad = (step_grad * jax.nn.sigmoid(raw_steps)).astype(bf16)

    tp = lax.axis_size("tp")
    maps = jnp.concatenate([local_b + bgrad, local_c], axis=1).astype(bf16)
    maps = lax.all_to_all(maps.reshape(tp, length // tp, 2 * STATE), "tp", 0, 0)
    grad_maps = jnp.sum(maps.astype(f32), axis=0)

    gathered = lax.all_gather(dt_grad, "tp", axis=0, tiled=True)
    replicas = lax.axis_size("dp") * count
    product = jnp.dot(gathered, layer_in[0], preferred_element_type=f32).astype(bf16)
    product = product.reshape(replicas, gathered.shape[0] // replicas, width)
    summed = jnp.sum(lax.all_to_all(product, ("dp", "ctx"), 0, 0).astype(f32), axis=0)
    squares = jnp.sum(summed * summed, axis=1)
    own_norm = jnp.sqrt(lax.psum(squares, "tp") + epsilon)
    target = jnp.sum(lax.all_gather(own_norm, ("dp", "ctx"))) / gathered.shape[0]
    grad_dt_proj = summed * jnp.minimum(1.0, target / own_norm)[:, None]
    return (grad_x[None], grad_maps[None], grad_dt_proj)


def mm_high(a, b, precision):
    return lax.dot_general(a, b, (((1,), (1,)), ((), ())), precision=precision, preferred_element_type=f32)


def solution(mesh):
    in_specs = (
        P("dp", "ctx", "tp"),
        P("dp", "ctx", "tp"),
        P("dp", "ctx", None),
        P("dp", "tp", "ctx"),
        P("tp"),
        P("dp", "ctx", "tp", None, None),
        P("dp", "ctx", "tp"),
        P("dp", None),
    )
    out_specs = (P("dp", "ctx", "tp"), P("dp", ("ctx", "tp"), None), P(("dp", "ctx"), "tp"))
    return jax.shard_map(shards, mesh=mesh, in_specs=in_specs, out_specs=out_specs, check_vma=False)
```

```python
import functools

import jax
import jax.numpy as jnp
from jax import lax
from jax.experimental import pallas as pl
from jax.experimental.pallas import tpu as pltpu
from jax.sharding import PartitionSpec as P

HEAD_DIM = 64
STATE = 128
PAIR = 2 * HEAD_DIM
TILE = 256
CHUNK = 64
epsilon = 1e-06
LOG2E = 1.4426950408889634
f32, bf16 = jnp.float32, jnp.bfloat16


def mm(a, b, ca, cb):
    return lax.dot_general(a, b, (((ca,), (cb,)), ((), ())), preferred_element_type=f32)


def spread(rows):
    heads = rows.shape[0]
    high = rows.astype(bf16).astype(f32)
    both = jnp.concatenate([high, rows - high], axis=0).astype(bf16)
    row = lax.broadcasted_iota(jnp.int32, (2 * heads, heads * HEAD_DIM), 0) % heads
    head = lax.broadcasted_iota(jnp.int32, (2 * heads, heads * HEAD_DIM), 1) // HEAD_DIM
    return mm(both, jnp.where(row == head, 1.0, 0.0).astype(bf16), 0, 0)


def head_sums(value, first):
    width = value.shape[1]
    high = value.astype(bf16)
    low = (value - high.astype(f32)).astype(bf16)
    row = lax.broadcasted_iota(jnp.int32, (2 * width, 128), 0) % width
    col = lax.broadcasted_iota(jnp.int32, (2 * width, 128), 1)
    chosen = jnp.where(col == first + row // HEAD_DIM, 1.0, 0.0).astype(bf16)
    return mm(jnp.concatenate([high, low], axis=1), chosen, 1, 0)


def enter_kernel(pairs, aux_ref, dy_ref, c_ref, s_ref, local_ref, sterm_ref, eo_ref):
    step = pl.program_id(0)

    @pl.when(step == 0)
    def _():
        sterm_ref[...] = jnp.zeros_like(sterm_ref)
        eo_ref[...] = jnp.zeros_like(eo_ref)

    c_rows = c_ref[...]
    enter = jnp.concatenate([aux_ref[p][6:8] for p in range(pairs)], axis=0)
    wide = dy_ref[...].astype(f32) * spread(enter)
    scaled = wide.astype(bf16)
    local_ref[...] = mm(c_rows, scaled, 0, 0).T.astype(bf16)
    state = s_ref[...].astype(bf16)
    sterm_ref[...] += mm(scaled, state, 1, 0)
    eo_ref[...] += head_sums(wide * mm(c_rows, state, 1, 1), step * 2 * pairs)


def quad_kernel(
    pairs, aux_ref, x_ref, dy_ref, b_ref, c_ref, labr_ref, labc_ref, *refs
):
    min_ref = refs[0] if len(refs) > 4 else None
    r_ref, a_ref, msum_ref, cb_ref = refs[-4:]
    length = x_ref.shape[0]

    @pl.when(pl.program_id(0) == 0)
    def _():
        at_j = lax.broadcasted_iota(jnp.int32, (length, length), 0)
        at_i = lax.broadcasted_iota(jnp.int32, (length, length), 1)
        keep = (at_i >= at_j) & (labc_ref[...] == labr_ref[...])
        cb_ref[...] = jnp.where(keep, mm(b_ref[...], c_ref[...], 1, 1), 0.0)
        msum_ref[...] = jnp.zeros_like(msum_ref) if min_ref is None else min_ref[...]

    blocks = length // TILE
    lane = lax.broadcasted_iota(jnp.int32, (length, PAIR), 1)
    for p in range(pairs):
        at = slice(p * PAIR, (p + 1) * PAIR)
        aux = aux_ref[p]
        cols = aux.T
        x = x_ref[:, at]
        dy = dy_ref[:, at]
        zero = jnp.zeros_like(dy)
        dys = (jnp.where(lane < HEAD_DIM, dy, zero), jnp.where(lane < HEAD_DIM, zero, dy))
        sums = [[jnp.zeros((8, TILE), f32) for _ in range(blocks)] for _ in range(2)]
        for jb in range(blocks):
            j0 = jb * TILE
            weights, sources = [], []
            for ib in range(jb, blocks):
                i0 = ib * TILE
                inner = [mm(x[j0 : j0 + TILE], dys[s][i0 : i0 + TILE], 1, 1) for s in range(2)]
                pieces = [[], []]
                for c in range(TILE // CHUNK):
                    lo = c * CHUNK
                    rows = slice(j0 + lo, j0 + lo + CHUNK)
                    cb = cb_ref[rows, i0 : i0 + TILE]
                    total = None
                    for s in range(2):
                        power = aux[s : s + 1, i0 : i0 + TILE] - cols[rows, 2 + s : 3 + s]
                        if ib == jb:
                            power = jnp.minimum(power, 16.0)
                        decay = jnp.exp2(power)
                        pieces[s].append((decay * cb).astype(bf16))
                        mixed = decay * inner[s][lo : lo + CHUNK]
                        total = mixed if total is None else total + mixed
                        product = (mixed * cb).reshape(CHUNK // 8, 8, TILE)
                        sums[s][ib] = sums[s][ib] + jnp.sum(product, axis=0)
                    msum_ref[rows, i0 : i0 + TILE] += total
                for s in range(2):
                    weights.append(jnp.concatenate(pieces[s], axis=0))
                    sources.append(dys[s][i0 : i0 + TILE])
            r_ref[j0 : j0 + TILE, at] = mm(
                jnp.concatenate(weights, axis=1), jnp.concatenate(sources, axis=0), 1, 0
            )
        for s in range(2):
            for ib in range(blocks):
                a_ref[0, 2 * p + s : 2 * p + s + 1, ib * TILE : (ib + 1) * TILE] = jnp.sum(
                    sums[s][ib], axis=0, keepdims=True
                )


def leave_kernel(
    pairs, aux_ref, x_ref, r_ref, b_ref, carry_ref, s_ref, gx_ref, u_ref, bgrad_ref, vw_ref
):
    step = pl.program_id(0)

    @pl.when(step == 0)
    def _():
        u_ref[...] = jnp.zeros_like(u_ref)
        bgrad_ref[...] = jnp.zeros_like(bgrad_ref)

    weight = spread(jnp.concatenate([aux_ref[p][4:6] for p in range(pairs)], axis=0))
    carry = carry_ref[...]
    x = x_ref[...].astype(f32)
    after = weight * mm(b_ref[...], carry, 1, 1)
    grad = r_ref[...] + after
    gx_ref[...] = grad.astype(bf16)
    u_ref[...] += head_sums(x * grad, step * 2 * pairs)
    bgrad_ref[...] += mm((weight * x).astype(bf16), carry, 1, 0)
    w_sums = jnp.sum(x * after, axis=0, keepdims=True)
    both = carry.astype(f32) * s_ref[...]
    for p in range(pairs):
        first, last = p * PAIR, p * PAIR + HEAD_DIM
        vw_ref[p, 0:1, :] = jnp.sum(both[first : first + HEAD_DIM], axis=0, keepdims=True)
        vw_ref[p, 1:2, :] = jnp.sum(both[last : last + HEAD_DIM], axis=0, keepdims=True)
        vw_ref[p, 2:3, :] = w_sums[:, first : first + PAIR]
        vw_ref[p, 3:8, :] = jnp.zeros((5, STATE), f32)


def finish_kernel(
    sizes, heads, prod_ref, maps_ref, out_ref, gmaps_ref,
    land, mland, sq, sq_land, nrm, nrm_land,
    send, recv, msend, mrecv, qsend, qrecv, nsend, nrecv,
):
    dp, ctx, tp = sizes
    replicas = dp * ctx
    my_tp = lax.axis_index("tp")
    my_ctx = lax.axis_index("ctx")
    my_dp = lax.axis_index("dp")
    me = my_dp * ctx + my_ctx

    def replica(offset):
        return lax.rem(me + offset, replicas)

    def place(other):
        return (other // ctx, lax.rem(other, ctx), my_tp)

    def beside(offset):
        return (my_dp, my_ctx, lax.rem(my_tp + offset, tp))

    barrier = pltpu.get_barrier_semaphore()
    for o in range(1, replicas):
        pl.semaphore_signal(
            barrier, inc=1, device_id=place(replica(o)), device_id_type=pl.DeviceIdType.MESH
        )
    for o in range(1, tp):
        pl.semaphore_signal(
            barrier, inc=1, device_id=beside(o), device_id_type=pl.DeviceIdType.MESH
        )
    pl.semaphore_wait(barrier, replicas - 1 + tp - 1)

    def copy(src, dst, sends, recvs, o, to):
        made = pltpu.make_async_remote_copy(
            src_ref=src,
            dst_ref=dst,
            send_sem=sends.at[o - 1],
            recv_sem=recvs.at[o - 1],
            device_id=to,
            device_id_type=pl.DeviceIdType.MESH,
        )
        made.start()
        return made

    big = []
    for o in range(1, replicas):
        other = replica(o)
        big.append(copy(prod_ref.at[other], land.at[o - 1], send, recv, o, place(other)))
    small = []
    for o in range(1, tp):
        target = lax.rem(my_tp + o, tp)
        small.append(copy(maps_ref.at[target], mland.at[o - 1], msend, mrecv, o, beside(o)))
    gmaps = maps_ref[my_tp].astype(f32)
    for o in range(1, tp):
        small[o - 1].wait_recv()
        gmaps = gmaps + mland[o - 1].astype(f32)
    gmaps_ref[...] = gmaps
    total = prod_ref[me].astype(f32)
    for o in range(1, replicas):
        big[o - 1].wait_recv()
        total = total + land[o - 1].astype(f32)
    square = jnp.sum(total * total, axis=1, keepdims=True)
    square = jnp.broadcast_to(square, sq.shape)
    sq[...] = square
    squares = [copy(sq, sq_land.at[o - 1], qsend, qrecv, o, beside(o)) for o in range(1, tp)]
    for o in range(1, tp):
        squares[o - 1].wait_recv()
        square = square + sq_land[o - 1]
    rows = out_ref.shape[0]
    splits = total.shape[0] // rows
    norm = square[:rows]
    for k in range(1, splits):
        norm = norm + square[k * rows : (k + 1) * rows]
    norm = jnp.sqrt(norm + epsilon)
    norm_sum = jnp.broadcast_to(jnp.sum(norm, axis=0, keepdims=True), nrm.shape)
    nrm[...] = norm_sum
    norms = [copy(nrm, nrm_land.at[o - 1], nsend, nrecv, o, place(replica(o))) for o in range(1, replicas)]
    for o in range(1, replicas):
        norms[o - 1].wait_recv()
        norm_sum = norm_sum + nrm_land[o - 1]
    scale = jnp.minimum(1.0, norm_sum[0:1] / heads / norm)[:, 0:1]
    columns = total.shape[1]
    for k in range(splits):
        out_ref[:, k * columns : (k + 1) * columns] = total[k * rows : (k + 1) * rows] * scale
    for made in big + small + squares + norms:
        made.wait_send()


def segments(lengths_row, anchor, length):
    doc_ends = jnp.cumsum(lengths_row)
    positions = anchor + jnp.arange(length, dtype=jnp.int32)
    labels = jnp.sum((positions[:, None] >= doc_ends[None, :]).astype(jnp.int32), axis=1)
    before = jnp.sum((anchor - 1 >= doc_ends).astype(jnp.int32))
    before = jnp.where(anchor > 0, before, -1)
    return (labels, before)


def full(shape):
    return pl.BlockSpec(shape, lambda g: (0,) * len(shape))


def shift(value, back, count):
    if back >= count:
        return jax.tree.map(jnp.zeros_like, value)
    moves = [(k, k - back) for k in range(back, count)]
    return jax.tree.map(lambda part: lax.ppermute(part, "ctx", moves), value)


def shards(x_in, grad_out, state_maps, dt_raw, a_log, saved_states, layer_in, doc_lengths):
    high = lax.Precision.HIGHEST
    length, width = x_in.shape[1:]
    head_count = a_log.shape[0]
    pair_count = head_count // 2
    x_rows, dy_rows = x_in[0], grad_out[0]
    b_half = state_maps[0, :, :STATE]
    c_half = state_maps[0, :, STATE:]
    raw_steps = dt_raw[0]
    states = saved_states.reshape(width, STATE)
    count = lax.axis_size("ctx")
    anchor = lax.axis_index("ctx") * length
    labels, before = segments(doc_lengths[0], anchor, length)
    positions = jnp.arange(length)
    upto = (positions[:, None] <= positions[None, :]).astype(f32)
    steps = jax.nn.softplus(raw_steps)
    decay_rate = -jnp.exp(a_log)
    cumulative = jnp.dot(decay_rate[:, None] * steps, upto, precision=high)
    enter_w = jnp.exp(cumulative) * (labels == before).astype(f32)[None, :]
    leave_w = jnp.exp(cumulative[:, -1:] - cumulative) * (labels == labels[-1]).astype(f32)[None, :]
    scaled_cum = cumulative * LOG2E
    aux = jnp.stack([scaled_cum, scaled_cum - jnp.log2(steps), steps * leave_w, enter_w])
    aux = aux.reshape(4, pair_count, 2, length).transpose(1, 0, 2, 3)
    aux = aux.reshape(pair_count, 8, length)
    ends = enter_w[:, -1]

    wide_pairs = 4
    groups = pair_count // wide_pairs
    aux_spec = pl.BlockSpec((wide_pairs, 8, length), lambda g: (g, 0, 0))
    col_spec = pl.BlockSpec((length, wide_pairs * PAIR), lambda g: (0, g))
    row_spec = pl.BlockSpec((wide_pairs * PAIR, STATE), lambda g: (g, 0))
    limit = pltpu.CompilerParams(vmem_limit_bytes=40 * 1024 * 1024)
    local, state_term, enter_out = pl.pallas_call(
        functools.partial(enter_kernel, wide_pairs),
        grid=(groups,),
        in_specs=[aux_spec, col_spec, full((length, STATE)), row_spec],
        out_specs=[row_spec, full((length, STATE)), full((length, 128))],
        out_shape=[
            jax.ShapeDtypeStruct((width, STATE), bf16),
            jax.ShapeDtypeStruct((length, STATE), f32),
            jax.ShapeDtypeStruct((length, 128), f32),
        ],
        compiler_params=limit,
        name="enter",
    )(aux, dy_rows, c_half, states)

    odd = lax.axis_index("ctx") % 2
    half = head_count // 2
    swap = [(k, k ^ 1) for k in range(count)]

    def take(value, which):
        return lax.dynamic_index_in_dim(value, which, 0, keepdims=False)

    whole_local = local.reshape(2, half, HEAD_DIM * STATE)
    half_ends = ends.reshape(2, half)
    mine, mine_end = take(whole_local, odd), take(half_ends, odd)
    other = lax.ppermute(take(whole_local, 1 - odd), "ctx", swap)
    other_end = lax.ppermute(take(half_ends, 1 - odd), "ctx", swap)
    first = jnp.where(odd == 0, mine, other).astype(f32)
    second = jnp.where(odd == 0, other, mine).astype(f32)
    first_end = jnp.where(odd == 0, mine_end, other_end)
    group = (first + first_end[:, None] * second).astype(bf16)
    group_end = mine_end * other_end
    reach, window = 1, max(count // 4, 1)
    while reach < window:
        ahead, ahead_end = shift((group, group_end), 2 * reach, count)
        group = (group.astype(f32) + group_end[:, None] * ahead.astype(f32)).astype(bf16)
        group_end = group_end * ahead_end
        reach *= 2
    after = shift(group, 2, count)
    even_end = jnp.where(odd == 0, other_end, mine_end)
    even_after = (second + even_end[:, None] * after.astype(f32)).astype(bf16)
    back = lax.ppermute(jnp.where(odd == 0, after, even_after), "ctx", swap)
    kept = jnp.where(odd == 0, even_after, after)
    carry = jnp.where(odd == 0, jnp.stack([kept, back]), jnp.stack([back, kept]))
    carry = carry.reshape(width, STATE)

    quad_pairs = 2
    parts = 4 if pair_count % (4 * quad_pairs) == 0 else 1
    quad_groups = pair_count // quad_pairs // parts
    labr, labc = labels[None, :], labels[:, None]
    mixed = r_local = None
    a_parts = []
    for part in range(parts):
        base = part * quad_groups
        quad_spec = pl.BlockSpec((length, quad_pairs * PAIR), lambda g, base=base: (0, base + g))
        r_local, a_part, mixed = pl.pallas_call(
            functools.partial(quad_kernel, quad_pairs),
            grid=(quad_groups,),
            in_specs=[
                pl.BlockSpec((quad_pairs, 8, length), lambda g, base=base: (base + g, 0, 0)),
                quad_spec,
                quad_spec,
                full((length, STATE)),
                full((length, STATE)),
                full((1, length)),
                full((length, 1)),
            ]
            + ([full((length, length)), pl.BlockSpec(memory_space=pl.ANY)] if part else []),
            out_specs=[
                quad_spec,
                pl.BlockSpec((1, 2 * quad_pairs, length), lambda g: (g, 0, 0)),
                full((length, length)),
            ],
            out_shape=[
                jax.ShapeDtypeStruct((length, width), f32),
                jax.ShapeDtypeStruct((quad_groups, 2 * quad_pairs, length), f32),
                jax.ShapeDtypeStruct((length, length), f32),
            ],
            scratch_shapes=[pltpu.VMEM((length, length), f32)],
            input_output_aliases={8: 0} if part else {},
            compiler_params=limit,
            cost_estimate=pl.CostEstimate(
                flops=50_000_000_000 // parts, bytes_accessed=20_000_000 // parts, transcendentals=0
            ),
            name="quad",
        )(aux, x_rows, dy_rows, b_half, c_half, labr, labc, *([mixed, r_local] if part else []))
        a_parts.append(a_part.reshape(-1, length))
    a_sum = jnp.concatenate(a_parts, axis=0)
    keep = (positions[:, None] <= positions[None, :]) & (labc == labr)
    mixed = jnp.where(keep, mixed, 0.0).astype(bf16)
    local_b = jnp.dot(mixed, c_half, preferred_element_type=f32)
    local_c = mm(mixed, b_half, 0, 0) + state_term

    grad_x, u_sum, bgrad, vw = pl.pallas_call(
        functools.partial(leave_kernel, wide_pairs),
        grid=(groups,),
        in_specs=[aux_spec, col_spec, col_spec, full((length, STATE)), row_spec, row_spec],
        out_specs=[
            col_spec,
            full((length, 128)),
            full((length, STATE)),
            pl.BlockSpec((wide_pairs, 8, STATE), lambda g: (g, 0, 0)),
        ],
        out_shape=[
            jax.ShapeDtypeStruct((length, width), bf16),
            jax.ShapeDtypeStruct((length, 128), f32),
            jax.ShapeDtypeStruct((length, STATE), f32),
            jax.ShapeDtypeStruct((pair_count, 8, STATE), f32),
        ],
        compiler_params=limit,
        name="leave",
    )(aux, x_rows, r_local, b_half, carry, states)
    v_term = ends * jnp.sum(vw[:, 0:2], axis=2).reshape(head_count)
    w_sum = jnp.sum(vw[:, 2].reshape(head_count, HEAD_DIM), axis=1)
    u_rows = u_sum[:, :head_count].T
    cum_grad = a_sum + enter_out[:, :head_count].T - u_rows
    tail_sum = mm_high(cum_grad, upto, high) + (v_term + w_sum)[:, None]
    step_grad = u_rows / steps + decay_rate[:, None] * tail_sum
    dt_grad = (step_grad * jax.nn.sigmoid(raw_steps)).astype(bf16)

    sizes = (lax.axis_size("dp"), count, lax.axis_size("tp"))
    tp, replicas = sizes[2], sizes[0] * count
    maps = jnp.concatenate([local_b + bgrad, local_c], axis=1).astype(bf16)
    maps = maps.reshape(tp, length // tp, 2 * STATE)
    gathered = lax.all_gather(dt_grad, "tp", axis=0, tiled=True)
    rows = gathered.shape[0] // replicas
    splits = max(16 // rows, 1)
    columns = width // splits
    product = jnp.concatenate(
        [
            jnp.dot(
                gathered,
                layer_in[0, :, k * columns : (k + 1) * columns],
                preferred_element_type=f32,
            ).astype(bf16).reshape(replicas, rows, columns)
            for k in range(splits)
        ],
        axis=1,
    )
    piece = (splits * rows, columns)
    vmem = pl.BlockSpec(memory_space=pltpu.VMEM)
    sems = pltpu.SemaphoreType.DMA
    grad_dt_proj, grad_maps = pl.pallas_call(
        functools.partial(finish_kernel, sizes, gathered.shape[0]),
        in_specs=[vmem, vmem],
        out_specs=[vmem, vmem],
        out_shape=[
            jax.ShapeDtypeStruct((rows, width), f32),
            jax.ShapeDtypeStruct((length // tp, 2 * STATE), f32),
        ],
        scratch_shapes=[
            pltpu.VMEM((replicas - 1,) + piece, bf16),
            pltpu.VMEM((tp - 1, length // tp, 2 * STATE), bf16),
            pltpu.VMEM((piece[0], 128), f32),
            pltpu.VMEM((tp - 1, piece[0], 128), f32),
            pltpu.VMEM((8, 128), f32),
            pltpu.VMEM((replicas - 1, 8, 128), f32),
            sems((replicas - 1,)),
            sems((replicas - 1,)),
            sems((tp - 1,)),
            sems((tp - 1,)),
            sems((tp - 1,)),
            sems((tp - 1,)),
            sems((replicas - 1,)),
            sems((replicas - 1,)),
        ],
        compiler_params=pltpu.CompilerParams(
            collective_id=0, has_side_effects=True, vmem_limit_bytes=40 * 1024 * 1024
        ),
        name="finish",
    )(product, maps)
    return (grad_x[None], grad_maps[None], grad_dt_proj)


def mm_high(a, b, precision):
    return lax.dot_general(a, b, (((1,), (1,)), ((), ())), precision=precision, preferred_element_type=f32)


def solution(mesh):
    in_specs = (
        P("dp", "ctx", "tp"),
        P("dp", "ctx", "tp"),
        P("dp", "ctx", None),
        P("dp", "tp", "ctx"),
        P("tp"),
        P("dp", "ctx", "tp", None, None),
        P("dp", "ctx", "tp"),
        P("dp", None),
    )
    out_specs = (P("dp", "ctx", "tp"), P("dp", ("ctx", "tp"), None), P(("dp", "ctx"), "tp"))
    return jax.shard_map(shards, mesh=mesh, in_specs=in_specs, out_specs=out_specs, check_vma=False)
```

```python
import functools

import jax
import jax.numpy as jnp
from jax import lax
from jax.experimental import pallas as pl
from jax.experimental.pallas import tpu as pltpu
from jax.sharding import PartitionSpec as P

HEAD_DIM = 64
STATE = 128
PAIR = 2 * HEAD_DIM
TILE = 256
CHUNK = 64
epsilon = 1e-06
LOG2E = 1.4426950408889634
f32, bf16 = jnp.float32, jnp.bfloat16


def mm(a, b, ca, cb):
    return lax.dot_general(a, b, (((ca,), (cb,)), ((), ())), preferred_element_type=f32)


def spread(rows):
    heads = rows.shape[0]
    high = rows.astype(bf16).astype(f32)
    both = jnp.concatenate([high, rows - high], axis=0).astype(bf16)
    row = lax.broadcasted_iota(jnp.int32, (2 * heads, heads * HEAD_DIM), 0) % heads
    head = lax.broadcasted_iota(jnp.int32, (2 * heads, heads * HEAD_DIM), 1) // HEAD_DIM
    return mm(both, jnp.where(row == head, 1.0, 0.0).astype(bf16), 0, 0)


def head_sums(value, first):
    width = value.shape[1]
    high = value.astype(bf16)
    low = (value - high.astype(f32)).astype(bf16)
    row = lax.broadcasted_iota(jnp.int32, (2 * width, 128), 0) % width
    col = lax.broadcasted_iota(jnp.int32, (2 * width, 128), 1)
    chosen = jnp.where(col == first + row // HEAD_DIM, 1.0, 0.0).astype(bf16)
    return mm(jnp.concatenate([high, low], axis=1), chosen, 1, 0)


def enter_kernel(pairs, aux_ref, dy_ref, c_ref, s_ref, local_ref, sterm_ref, eo_ref):
    step = pl.program_id(0)

    @pl.when(step == 0)
    def _():
        sterm_ref[...] = jnp.zeros_like(sterm_ref)
        eo_ref[...] = jnp.zeros_like(eo_ref)

    c_rows = c_ref[...]
    enter = jnp.concatenate([aux_ref[p][6:8] for p in range(pairs)], axis=0)
    wide = dy_ref[...].astype(f32) * spread(enter)
    scaled = wide.astype(bf16)
    local_ref[...] = mm(c_rows, scaled, 0, 0).T.astype(bf16)
    state = s_ref[...].astype(bf16)
    sterm_ref[...] += mm(scaled, state, 1, 0)
    eo_ref[...] += head_sums(wide * mm(c_rows, state, 1, 1), step * 2 * pairs)


def quad_kernel(
    pairs, aux_ref, x_ref, dy_ref, b_ref, c_ref, labr_ref, labc_ref, *refs
):
    min_ref = refs[0] if len(refs) > 4 else None
    r_ref, a_ref, msum_ref, cb_ref = refs[-4:]
    length = x_ref.shape[0]

    @pl.when(pl.program_id(0) == 0)
    def _():
        at_j = lax.broadcasted_iota(jnp.int32, (length, length), 0)
        at_i = lax.broadcasted_iota(jnp.int32, (length, length), 1)
        keep = (at_i >= at_j) & (labc_ref[...] == labr_ref[...])
        cb_ref[...] = jnp.where(keep, mm(b_ref[...], c_ref[...], 1, 1), 0.0)
        msum_ref[...] = jnp.zeros_like(msum_ref) if min_ref is None else min_ref[...]

    blocks = length // TILE
    lane = lax.broadcasted_iota(jnp.int32, (length, PAIR), 1)
    for p in range(pairs):
        at = slice(p * PAIR, (p + 1) * PAIR)
        aux = aux_ref[p]
        cols = aux.T
        x = x_ref[:, at]
        dy = dy_ref[:, at]
        zero = jnp.zeros_like(dy)
        dys = (jnp.where(lane < HEAD_DIM, dy, zero), jnp.where(lane < HEAD_DIM, zero, dy))
        sums = [[jnp.zeros((8, TILE), f32) for _ in range(blocks)] for _ in range(2)]
        for jb in range(blocks):
            j0 = jb * TILE
            weights, sources = [], []
            for ib in range(jb, blocks):
                i0 = ib * TILE
                inner = [mm(x[j0 : j0 + TILE], dys[s][i0 : i0 + TILE], 1, 1) for s in range(2)]
                pieces = [[], []]
                for c in range(TILE // CHUNK):
                    lo = c * CHUNK
                    rows = slice(j0 + lo, j0 + lo + CHUNK)
                    cb = cb_ref[rows, i0 : i0 + TILE]
                    total = None
                    for s in range(2):
                        power = aux[s : s + 1, i0 : i0 + TILE] - cols[rows, 2 + s : 3 + s]
                        if ib == jb:
                            power = jnp.minimum(power, 16.0)
                        decay = jnp.exp2(power)
                        pieces[s].append((decay * cb).astype(bf16))
                        mixed = decay * inner[s][lo : lo + CHUNK]
                        total = mixed if total is None else total + mixed
                        product = (mixed * cb).reshape(CHUNK // 8, 8, TILE)
                        sums[s][ib] = sums[s][ib] + jnp.sum(product, axis=0)
                    msum_ref[rows, i0 : i0 + TILE] += total
                for s in range(2):
                    weights.append(jnp.concatenate(pieces[s], axis=0))
                    sources.append(dys[s][i0 : i0 + TILE])
            r_ref[j0 : j0 + TILE, at] = mm(
                jnp.concatenate(weights, axis=1), jnp.concatenate(sources, axis=0), 1, 0
            )
        for s in range(2):
            for ib in range(blocks):
                a_ref[0, 2 * p + s : 2 * p + s + 1, ib * TILE : (ib + 1) * TILE] = jnp.sum(
                    sums[s][ib], axis=0, keepdims=True
                )


def leave_kernel(
    pairs, aux_ref, x_ref, r_ref, b_ref, carry_ref, s_ref, gx_ref, u_ref, bgrad_ref, vw_ref
):
    step = pl.program_id(0)

    @pl.when(step == 0)
    def _():
        u_ref[...] = jnp.zeros_like(u_ref)
        bgrad_ref[...] = jnp.zeros_like(bgrad_ref)

    weight = spread(jnp.concatenate([aux_ref[p][4:6] for p in range(pairs)], axis=0))
    carry = carry_ref[...]
    x = x_ref[...].astype(f32)
    after = weight * mm(b_ref[...], carry, 1, 1)
    grad = r_ref[...] + after
    gx_ref[...] = grad.astype(bf16)
    u_ref[...] += head_sums(x * grad, step * 2 * pairs)
    bgrad_ref[...] += mm((weight * x).astype(bf16), carry, 1, 0)
    w_sums = jnp.sum(x * after, axis=0, keepdims=True)
    both = carry.astype(f32) * s_ref[...]
    for p in range(pairs):
        first, last = p * PAIR, p * PAIR + HEAD_DIM
        vw_ref[p, 0:1, :] = jnp.sum(both[first : first + HEAD_DIM], axis=0, keepdims=True)
        vw_ref[p, 1:2, :] = jnp.sum(both[last : last + HEAD_DIM], axis=0, keepdims=True)
        vw_ref[p, 2:3, :] = w_sums[:, first : first + PAIR]
        vw_ref[p, 3:8, :] = jnp.zeros((5, STATE), f32)


def finish_kernel(
    sizes, heads, prod_ref, maps_ref, out_ref, gmaps_ref,
    land, mland, sq, sq_land, nrm, nrm_land,
    send, recv, msend, mrecv, qsend, qrecv, nsend, nrecv,
):
    dp, ctx, tp = sizes
    replicas = dp * ctx
    my_tp = lax.axis_index("tp")
    my_ctx = lax.axis_index("ctx")
    my_dp = lax.axis_index("dp")
    me = my_dp * ctx + my_ctx

    def replica(offset):
        return lax.rem(me + offset, replicas)

    def place(other):
        return (other // ctx, lax.rem(other, ctx), my_tp)

    def beside(offset):
        return (my_dp, my_ctx, lax.rem(my_tp + offset, tp))

    barrier = pltpu.get_barrier_semaphore()
    for o in range(1, replicas):
        pl.semaphore_signal(
            barrier, inc=1, device_id=place(replica(o)), device_id_type=pl.DeviceIdType.MESH
        )
    for o in range(1, tp):
        pl.semaphore_signal(
            barrier, inc=1, device_id=beside(o), device_id_type=pl.DeviceIdType.MESH
        )
    pl.semaphore_wait(barrier, replicas - 1 + tp - 1)

    def copy(src, dst, sends, recvs, o, to):
        made = pltpu.make_async_remote_copy(
            src_ref=src,
            dst_ref=dst,
            send_sem=sends.at[o - 1],
            recv_sem=recvs.at[o - 1],
            device_id=to,
            device_id_type=pl.DeviceIdType.MESH,
        )
        made.start()
        return made

    big = []
    for o in range(1, replicas):
        other = replica(o)
        big.append(copy(prod_ref.at[other], land.at[o - 1], send, recv, o, place(other)))
    small = []
    for o in range(1, tp):
        target = lax.rem(my_tp + o, tp)
        small.append(copy(maps_ref.at[target], mland.at[o - 1], msend, mrecv, o, beside(o)))
    gmaps = maps_ref[my_tp].astype(f32)
    for o in range(1, tp):
        small[o - 1].wait_recv()
        gmaps = gmaps + mland[o - 1].astype(f32)
    gmaps_ref[...] = gmaps
    total = prod_ref[me].astype(f32)
    for o in range(1, replicas):
        big[o - 1].wait_recv()
        total = total + land[o - 1].astype(f32)
    square = jnp.sum(total * total, axis=1, keepdims=True)
    square = jnp.broadcast_to(square, sq.shape)
    sq[...] = square
    squares = [copy(sq, sq_land.at[o - 1], qsend, qrecv, o, beside(o)) for o in range(1, tp)]
    for o in range(1, tp):
        squares[o - 1].wait_recv()
        square = square + sq_land[o - 1]
    rows = out_ref.shape[0]
    splits = total.shape[0] // rows
    norm = square[:rows]
    for k in range(1, splits):
        norm = norm + square[k * rows : (k + 1) * rows]
    norm = jnp.sqrt(norm + epsilon)
    norm_sum = jnp.broadcast_to(jnp.sum(norm, axis=0, keepdims=True), nrm.shape)
    nrm[...] = norm_sum
    norms = [copy(nrm, nrm_land.at[o - 1], nsend, nrecv, o, place(replica(o))) for o in range(1, replicas)]
    for o in range(1, replicas):
        norms[o - 1].wait_recv()
        norm_sum = norm_sum + nrm_land[o - 1]
    scale = jnp.minimum(1.0, norm_sum[0:1] / heads / norm)[:, 0:1]
    columns = total.shape[1]
    for k in range(splits):
        out_ref[:, k * columns : (k + 1) * columns] = total[k * rows : (k + 1) * rows] * scale
    for made in big + small + squares + norms:
        made.wait_send()


def segments(lengths_row, anchor, length):
    doc_ends = jnp.cumsum(lengths_row)
    positions = anchor + jnp.arange(length, dtype=jnp.int32)
    labels = jnp.sum((positions[:, None] >= doc_ends[None, :]).astype(jnp.int32), axis=1)
    before = jnp.sum((anchor - 1 >= doc_ends).astype(jnp.int32))
    before = jnp.where(anchor > 0, before, -1)
    return (labels, before)


def full(shape):
    return pl.BlockSpec(shape, lambda g: (0,) * len(shape))


def shift(value, back, count):
    if back >= count:
        return jax.tree.map(jnp.zeros_like, value)
    moves = [(k, k - back) for k in range(back, count)]
    return jax.tree.map(lambda part: lax.ppermute(part, "ctx", moves), value)


def shards(x_in, grad_out, state_maps, dt_raw, a_log, saved_states, layer_in, doc_lengths):
    high = lax.Precision.HIGHEST
    length, width = x_in.shape[1:]
    head_count = a_log.shape[0]
    pair_count = head_count // 2
    x_rows, dy_rows = x_in[0], grad_out[0]
    b_half = state_maps[0, :, :STATE]
    c_half = state_maps[0, :, STATE:]
    raw_steps = dt_raw[0]
    states = saved_states.reshape(width, STATE)
    count = lax.axis_size("ctx")
    anchor = lax.axis_index("ctx") * length
    labels, before = segments(doc_lengths[0], anchor, length)
    positions = jnp.arange(length)
    upto = (positions[:, None] <= positions[None, :]).astype(f32)
    steps = jax.nn.softplus(raw_steps)
    decay_rate = -jnp.exp(a_log)
    cumulative = jnp.dot(decay_rate[:, None] * steps, upto, precision=high)
    enter_w = jnp.exp(cumulative) * (labels == before).astype(f32)[None, :]
    leave_w = jnp.exp(cumulative[:, -1:] - cumulative) * (labels == labels[-1]).astype(f32)[None, :]
    scaled_cum = cumulative * LOG2E
    aux = jnp.stack([scaled_cum, scaled_cum - jnp.log2(steps), steps * leave_w, enter_w])
    aux = aux.reshape(4, pair_count, 2, length).transpose(1, 0, 2, 3)
    aux = aux.reshape(pair_count, 8, length)
    ends = enter_w[:, -1]

    wide_pairs = 4
    groups = pair_count // wide_pairs
    aux_spec = pl.BlockSpec((wide_pairs, 8, length), lambda g: (g, 0, 0))
    col_spec = pl.BlockSpec((length, wide_pairs * PAIR), lambda g: (0, g))
    row_spec = pl.BlockSpec((wide_pairs * PAIR, STATE), lambda g: (g, 0))
    limit = pltpu.CompilerParams(vmem_limit_bytes=56 * 1024 * 1024)
    local, state_term, enter_out = pl.pallas_call(
        functools.partial(enter_kernel, wide_pairs),
        grid=(groups,),
        in_specs=[aux_spec, col_spec, full((length, STATE)), row_spec],
        out_specs=[row_spec, full((length, STATE)), full((length, 128))],
        out_shape=[
            jax.ShapeDtypeStruct((width, STATE), bf16),
            jax.ShapeDtypeStruct((length, STATE), f32),
            jax.ShapeDtypeStruct((length, 128), f32),
        ],
        compiler_params=limit,
        name="enter",
    )(aux, dy_rows, c_half, states)

    odd = lax.axis_index("ctx") % 2
    half = head_count // 2
    swap = [(k, k ^ 1) for k in range(count)]

    def take(value, which):
        return lax.dynamic_index_in_dim(value, which, 0, keepdims=False)

    whole_local = local.reshape(2, half, HEAD_DIM, STATE)
    half_ends = ends.reshape(2, half)
    mine, mine_end = take(whole_local, odd), take(half_ends, odd)
    other = lax.ppermute(take(whole_local, 1 - odd), "ctx", swap)
    other_end = lax.ppermute(take(half_ends, 1 - odd), "ctx", swap)
    first = jnp.where(odd == 0, mine, other).astype(f32)
    second = jnp.where(odd == 0, other, mine).astype(f32)
    first_end = jnp.where(odd == 0, mine_end, other_end)
    group = (first + first_end[:, None, None] * second).astype(bf16)
    group_end = mine_end * other_end
    reach, window = 1, max(count // 4, 1)
    while reach < window:
        ahead, ahead_end = shift((group, group_end), 2 * reach, count)
        group = (group.astype(f32) + group_end[:, None, None] * ahead.astype(f32)).astype(bf16)
        group_end = group_end * ahead_end
        reach *= 2
    after = shift(group, 2, count)
    even_end = jnp.where(odd == 0, other_end, mine_end)
    even_after = (second + even_end[:, None, None] * after.astype(f32)).astype(bf16)
    back = lax.ppermute(jnp.where(odd == 0, after, even_after), "ctx", swap)
    kept = jnp.where(odd == 0, even_after, after)
    carry = jnp.where(odd == 0, jnp.stack([kept, back]), jnp.stack([back, kept]))
    carry = carry.reshape(width, STATE)

    quad_pairs = 2
    parts = 4 if pair_count % (4 * quad_pairs) == 0 else 1
    quad_groups = pair_count // quad_pairs // parts
    labr, labc = labels[None, :], labels[:, None]
    mixed = r_local = None
    a_parts = []
    for part in range(parts):
        base = part * quad_groups
        quad_spec = pl.BlockSpec((length, quad_pairs * PAIR), lambda g, base=base: (0, base + g))
        r_local, a_part, mixed = pl.pallas_call(
            functools.partial(quad_kernel, quad_pairs),
            grid=(quad_groups,),
            in_specs=[
                pl.BlockSpec((quad_pairs, 8, length), lambda g, base=base: (base + g, 0, 0)),
                quad_spec,
                quad_spec,
                full((length, STATE)),
                full((length, STATE)),
                full((1, length)),
                full((length, 1)),
            ]
            + ([full((length, length)), pl.BlockSpec(memory_space=pl.ANY)] if part else []),
            out_specs=[
                quad_spec,
                pl.BlockSpec((1, 2 * quad_pairs, length), lambda g: (g, 0, 0)),
                full((length, length)),
            ],
            out_shape=[
                jax.ShapeDtypeStruct((length, width), f32),
                jax.ShapeDtypeStruct((quad_groups, 2 * quad_pairs, length), f32),
                jax.ShapeDtypeStruct((length, length), f32),
            ],
            scratch_shapes=[pltpu.VMEM((length, length), f32)],
            input_output_aliases={8: 0} if part else {},
            compiler_params=limit,
            cost_estimate=pl.CostEstimate(
                flops=50_000_000_000 // parts, bytes_accessed=20_000_000 // parts, transcendentals=0
            ),
            name="quad",
        )(aux, x_rows, dy_rows, b_half, c_half, labr, labc, *([mixed, r_local] if part else []))
        a_parts.append(a_part.reshape(-1, length))
    a_sum = jnp.concatenate(a_parts, axis=0)
    keep = (positions[:, None] <= positions[None, :]) & (labc == labr)
    mixed = jnp.where(keep, mixed, 0.0).astype(bf16)
    local_b = jnp.dot(mixed, c_half, preferred_element_type=f32)
    local_c = mm(mixed, b_half, 0, 0) + state_term

    grad_x, u_sum, bgrad, vw = pl.pallas_call(
        functools.partial(leave_kernel, wide_pairs),
        grid=(groups,),
        in_specs=[aux_spec, col_spec, col_spec, full((length, STATE)), row_spec, row_spec],
        out_specs=[
            col_spec,
            full((length, 128)),
            full((length, STATE)),
            pl.BlockSpec((wide_pairs, 8, STATE), lambda g: (g, 0, 0)),
        ],
        out_shape=[
            jax.ShapeDtypeStruct((length, width), bf16),
            jax.ShapeDtypeStruct((length, 128), f32),
            jax.ShapeDtypeStruct((length, STATE), f32),
            jax.ShapeDtypeStruct((pair_count, 8, STATE), f32),
        ],
        compiler_params=limit,
        name="leave",
    )(aux, x_rows, r_local, b_half, carry, states)
    v_term = ends * jnp.sum(vw[:, 0:2], axis=2).reshape(head_count)
    w_sum = jnp.sum(vw[:, 2].reshape(head_count, HEAD_DIM), axis=1)
    u_rows = u_sum[:, :head_count].T
    cum_grad = a_sum + enter_out[:, :head_count].T - u_rows
    tail_sum = mm_high(cum_grad, upto, high) + (v_term + w_sum)[:, None]
    step_grad = u_rows / steps + decay_rate[:, None] * tail_sum
    dt_grad = (step_grad * jax.nn.sigmoid(raw_steps)).astype(bf16)

    sizes = (lax.axis_size("dp"), count, lax.axis_size("tp"))
    tp, replicas = sizes[2], sizes[0] * count
    maps = jnp.concatenate([local_b + bgrad, local_c], axis=1).astype(bf16)
    maps = maps.reshape(tp, length // tp, 2 * STATE)
    gathered = lax.all_gather(dt_grad, "tp", axis=0, tiled=True)
    rows = gathered.shape[0] // replicas
    splits = max(16 // rows, 1)
    columns = width // splits
    product = jnp.concatenate(
        [
            jnp.dot(
                gathered,
                layer_in[0, :, k * columns : (k + 1) * columns],
                preferred_element_type=f32,
            ).astype(bf16).reshape(replicas, rows, columns)
            for k in range(splits)
        ],
        axis=1,
    )
    piece = (splits * rows, columns)
    vmem = pl.BlockSpec(memory_space=pltpu.VMEM)
    sems = pltpu.SemaphoreType.DMA
    grad_dt_proj, grad_maps = pl.pallas_call(
        functools.partial(finish_kernel, sizes, gathered.shape[0]),
        in_specs=[vmem, vmem],
        out_specs=[vmem, vmem],
        out_shape=[
            jax.ShapeDtypeStruct((rows, width), f32),
            jax.ShapeDtypeStruct((length // tp, 2 * STATE), f32),
        ],
        scratch_shapes=[
            pltpu.VMEM((replicas - 1,) + piece, bf16),
            pltpu.VMEM((tp - 1, length // tp, 2 * STATE), bf16),
            pltpu.VMEM((piece[0], 128), f32),
            pltpu.VMEM((tp - 1, piece[0], 128), f32),
            pltpu.VMEM((8, 128), f32),
            pltpu.VMEM((replicas - 1, 8, 128), f32),
            sems((replicas - 1,)),
            sems((replicas - 1,)),
            sems((tp - 1,)),
            sems((tp - 1,)),
            sems((tp - 1,)),
            sems((tp - 1,)),
            sems((replicas - 1,)),
            sems((replicas - 1,)),
        ],
        compiler_params=pltpu.CompilerParams(
            collective_id=0, has_side_effects=True, vmem_limit_bytes=40 * 1024 * 1024
        ),
        name="finish",
    )(product, maps)
    return (grad_x[None], grad_maps[None], grad_dt_proj)


def mm_high(a, b, precision):
    return lax.dot_general(a, b, (((1,), (1,)), ((), ())), precision=precision, preferred_element_type=f32)


def solution(mesh):
    in_specs = (
        P("dp", "ctx", "tp"),
        P("dp", "ctx", "tp"),
        P("dp", "ctx", None),
        P("dp", "tp", "ctx"),
        P("tp"),
        P("dp", "ctx", "tp", None, None),
        P("dp", "ctx", "tp"),
        P("dp", None),
    )
    out_specs = (P("dp", "ctx", "tp"), P("dp", ("ctx", "tp"), None), P(("dp", "ctx"), "tp"))
    return jax.shard_map(shards, mesh=mesh, in_specs=in_specs, out_specs=out_specs, check_vma=False)
```
